32 devices in a mesh: sub: 4 (over y, x), beam: 8 (over z, core).
Axes of the slice: x: 2, y: 2, z: 4, core: 2. Of those that a mesh axis runs over, the one named last changes fastest.
Arguments:
- voltages: bfloat16 [1024, 256, 2, 1024], P(('sub', 'beam')), may hold values from -6 to 6
- weights: bfloat16 [256, 2, 1024, 1024], P(('sub', 'beam')), may hold values from -0.1875 to 0.1875
- antenna_map: int32 [1024], replicated, may hold values from 0 to 1023, each once
- delays: int32 [256, 32], P('sub'), may hold values from 0 to 127, as said below
Outputs:
- filterbank: bfloat16 [256, 1024, 256], P('sub', 'beam')
- series: float32 [32, 1024, 128], P('sub', 'beam')
The draws below stay inside these ranges and needn't reach their ends.
Inputs may be any that keep to these rules, and one draw needn't show every extreme that they name: antenna_map is a permutation of the antennas. delays never rise with the channel and never fall with the trial; trial 0 has no delay.
All inputs are finite; a program needn't handle non-finite values.
Results may differ from the reference program's by a relative error of at most 0.008.
Values may be sent and summed in bfloat16 or wider, within the bound.
A program may use at most 192 MiB of HBM per device.

```python
import math
import jax
import jax.numpy as jnp
from jax import lax

A = 1024
NFFT = 1024
C = 256
B = 1024
TRIALS = 32
MAXD = 128
OUT = 128
FR = 256


def draw_delays(key, part):
    inner = jax.random.randint(key, (TRIALS - 2,), 0, MAXD, dtype=jnp.int32)
    measures = jnp.sort(jnp.concatenate([jnp.zeros((1,), jnp.int32), inner, jnp.full((1,), MAXD - 1, jnp.int32)]))
    channel = jnp.arange(C, dtype=jnp.int32)
    curve = 2 ** 30 // ((C + channel) * (C + channel))
    return measures[None, :] * curve[:, None] // curve[0]


def level_of(key, extent, shards, smallest, largest):
    factor_of = 1.0
    for dim, shards_of in shards:
        heights = jax.random.uniform(jax.random.fold_in(jax.random.fold_in(key, 6), dim), (shards_of,), jnp.float32, smallest / len(shards), largest / len(shards))
        factor_of = factor_of * jnp.repeat(jnp.exp(heights), extent[dim] // shards_of).reshape((-1,) + (1,) * (len(extent) - 1 - dim))
    return factor_of


def gaussian(rng, shape, spread, bound, shards=(), held_as=jnp.bfloat16):
    result = spread * jax.random.normal(rng, shape, jnp.float32)
    if shards:
        result = result * level_of(rng, shape, shards, -0.22, 0.18)
    return jnp.clip(result, -bound, bound).astype(held_as)


def setup_inputs(seed: int = 0) -> dict:
    streams_of = jax.random.split(jax.random.key(seed), 5)
    voltages = gaussian(streams_of[0], (A, FR, 2, NFFT), 1.0, 6.0, ((0, 32),))
    weights = gaussian(streams_of[1], (C, 2, B, A), A ** -0.5, 0.1875, ((0, 32),))
    antenna_map = jax.random.permutation(streams_of[2], A).astype(jnp.int32)
    delays = draw_delays(jax.random.fold_in(streams_of[4], 71), 0)
    return dict(voltages=voltages, weights=weights, antenna_map=antenna_map, delays=delays)


def dft_table():
    sample = jnp.arange(NFFT, dtype=jnp.int32)
    channel = jnp.arange(C, dtype=jnp.int32)
    turns = channel[:, None] * sample[None, :] % NFFT
    phase = turns.astype(jnp.float32) * (2.0 * math.pi / NFFT)
    cosine = jnp.cos(phase) / math.sqrt(NFFT)
    sine = jnp.sin(phase) / math.sqrt(NFFT)
    real_row = jnp.stack([cosine, sine], axis=1)
    imag_row = jnp.stack([-sine, cosine], axis=1)
    return jnp.stack([real_row, imag_row], axis=0).astype(jnp.bfloat16)

def reference(voltages, weights, antenna_map, delays):
    table = dft_table().astype(jnp.float32)

    def channelize(block):
        return jnp.einsum('ocin,afin->aocf', table, block.astype(jnp.float32)).astype(jnp.bfloat16)
    spectra = lax.map(channelize, voltages.reshape(8, A // 8, FR, 2, NFFT)).reshape(A, 2, C, FR)
    by_channel = jnp.transpose(spectra, (2, 0, 1, 3))

    def form_beams(inputs):
        weight_chan, data_chan = inputs
        ordered = jnp.take(weight_chan, antenna_map, axis=2)
        beam_re = jnp.dot(ordered[0], data_chan[:, 0], preferred_element_type=jnp.float32) - jnp.dot(ordered[1], data_chan[:, 1], preferred_element_type=jnp.float32)
        beam_im = jnp.dot(ordered[0], data_chan[:, 1], preferred_element_type=jnp.float32) + jnp.dot(ordered[1], data_chan[:, 0], preferred_element_type=jnp.float32)
        return (beam_re * beam_re + beam_im * beam_im).astype(jnp.bfloat16)
    filterbank = lax.map(form_beams, (weights, by_channel))

    def add_channel(total, inputs):
        power_chan, delay_chan = inputs

        def shifted(delay_value):
            return lax.dynamic_slice_in_dim(power_chan, delay_value, OUT, 1)
        moved = jax.vmap(shifted)(delay_chan).astype(jnp.float32)
        return (total + moved, None)
    start_total = jnp.zeros((TRIALS, B, OUT), jnp.float32)
    total, unused = lax.scan(add_channel, start_total, (filterbank, delays))
    series = total * (1.0 / C)
    return (filterbank, series)
```

```python
import functools
import math

import jax
import jax.numpy as jnp
import numpy as np
from jax import lax
from jax.experimental import pallas as pl
from jax.experimental.pallas import tpu as pltpu
from jax.sharding import PartitionSpec as P

VMEM_BYTES = 48 * 1024 * 1024


def dft_rows(channels, samples):
    turns = (channels[:, None] * np.arange(samples)[None, :]) % samples
    phase = turns.astype(np.float32) * np.float32(2.0 * math.pi / samples)
    cosine = np.cos(phase) / math.sqrt(samples)
    sine = np.sin(phase) / math.sqrt(samples)
    real_row = np.stack([cosine, sine], axis=1)
    imag_row = np.stack([-sine, cosine], axis=1)
    return jnp.asarray(np.stack([real_row, imag_row], axis=1).astype(np.float32), jnp.bfloat16)


def beam_kernel(map_ref, x_ref, w_ref, out_ref, select, ordered):
    antennas = select.shape[0]
    frames = x_ref.shape[-1]

    @pl.when((pl.program_id(0) == 0) & (pl.program_id(1) == 0))
    def _():
        wanted = lax.broadcasted_iota(jnp.int32, (antennas, antennas), 0)
        select[...] = (wanted == map_ref[...]).astype(jnp.bfloat16)

    @pl.when(pl.program_id(1) == 0)
    def _():
        for part in range(2):
            rows = x_ref[:, 0, part].reshape(antennas, frames)
            ordered[:, part * frames:(part + 1) * frames] = jnp.dot(
                select[...], rows, preferred_element_type=jnp.float32
            ).astype(jnp.bfloat16)

    by_re = jnp.dot(w_ref[0, 0], ordered[...], preferred_element_type=jnp.float32)
    by_im = jnp.dot(w_ref[0, 1], ordered[...], preferred_element_type=jnp.float32)
    beam_re = by_re[:, :frames] - by_im[:, frames:]
    beam_im = by_re[:, frames:] + by_im[:, :frames]
    power = (beam_re * beam_re + beam_im * beam_im).astype(out_ref.dtype)
    out_ref[...] = power.reshape(out_ref.shape)


def form_beams(antenna_map, moved, weights, chunk, beam_count):
    senders, channels, _, local, frames = moved.shape
    antennas = senders * local
    beams = weights.shape[2]
    per_owner = beams // beam_count
    owners_step = max(1, 512 // per_owner)
    rows = owners_step * per_owner
    flops = channels * (2 * antennas * antennas * 2 * frames + 4 * beams * antennas * 2 * frames)
    nbytes = channels * (4 * beams * antennas + 4 * antennas * frames + 2 * beams * frames)
    return pl.pallas_call(
        beam_kernel,
        grid=(channels, beams // rows),
        in_specs=[
            pl.BlockSpec((1, antennas), lambda c, b: (0, 0)),
            pl.BlockSpec((senders, 1, 2, local, frames), lambda c, b: (0, c, 0, 0, 0)),
            pl.BlockSpec((1, 2, rows, antennas), lambda c, b: (chunk * channels + c, 0, b, 0)),
        ],
        out_specs=pl.BlockSpec((owners_step, 1, per_owner, frames), lambda c, b: (b, c, 0, 0)),
        out_shape=jax.ShapeDtypeStruct((beam_count, channels, per_owner, frames), jnp.bfloat16),
        scratch_shapes=[
            pltpu.VMEM((antennas, antennas), jnp.bfloat16),
            pltpu.VMEM((antennas, 2 * frames), jnp.bfloat16),
        ],
        compiler_params=pltpu.CompilerParams(vmem_limit_bytes=VMEM_BYTES),
        cost_estimate=pl.CostEstimate(flops=flops, bytes_accessed=nbytes, transcendentals=0),
        name="form_beams",
    )(antenna_map.reshape(1, antennas), moved, weights)


def dedisperse_kernel(scale, first, delays_ref, x_ref, *refs):
    if first:
        bank_ref, total_ref, turned = refs
        earlier = None
    else:
        earlier, _, bank_ref, total_ref, turned = refs
    senders, channels = x_ref.shape[:2]
    trials, out_frames = total_ref.shape[:2]
    bank_ref[:, 0] = x_ref[...]

    @pl.loop(0, senders)
    def _(sender):
        for channel in range(channels):
            turned[sender * channels + channel] = x_ref[sender, channel].astype(jnp.float32).T

    @pl.loop(0, trials)
    def _(trial):
        total = None if first else earlier[trial]
        for index in range(senders * channels):
            piece = turned[index, pl.ds(delays_ref[index, trial], out_frames), :]
            total = piece if total is None else total + piece
        if scale is not None:
            total = total * scale
        total_ref[trial] = total.astype(total_ref.dtype)


def dedisperse(delays, power, earlier, bank, chunk, chunks, out_frames, scale):
    senders, channels, beams, frames = power.shape
    trials = delays.shape[1]
    first = earlier is None
    whole = lambda: pl.BlockSpec(memory_space=pltpu.VMEM)
    bank_block = pl.BlockSpec((senders, 1, channels, beams, frames), lambda i: (0, chunk, 0, 0, 0))
    operands = [delays, power] + ([] if first else [earlier, bank])
    in_specs = [pl.BlockSpec(memory_space=pltpu.SMEM), whole()]
    if not first:
        in_specs += [whole(), pl.BlockSpec(memory_space=pl.ANY)]
    total_type = jnp.float32 if scale is None else jnp.bfloat16
    work = senders * channels * trials * out_frames * beams
    return pl.pallas_call(
        functools.partial(dedisperse_kernel, scale, first),
        grid=(1,),
        in_specs=in_specs,
        out_specs=[bank_block, whole()],
        out_shape=[
            jax.ShapeDtypeStruct((senders, chunks, channels, beams, frames), jnp.bfloat16),
            jax.ShapeDtypeStruct((trials, out_frames, beams), total_type),
        ],
        scratch_shapes=[pltpu.VMEM((senders * channels, frames, beams), jnp.float32)],
        input_output_aliases={} if first else {3: 0},
        compiler_params=pltpu.CompilerParams(vmem_limit_bytes=VMEM_BYTES),
        cost_estimate=pl.CostEstimate(flops=4 * work, bytes_accessed=4 * 1024 * 1024, transcendentals=0),
        name="dedisperse",
    )(*operands)


def on_device(voltages, weights, antenna_map, delays):
    samples = voltages.shape[3]
    sub_count = lax.axis_size("sub")
    beam_count = lax.axis_size("beam")
    devices = sub_count * beam_count
    owned = weights.shape[0]
    all_channels = owned * devices
    trials = delays.shape[1]
    out_frames = voltages.shape[1] // 2
    chunks = min(4, owned)
    per_chunk = owned // chunks
    first_of = np.arange(devices)[:, None] * owned + np.arange(per_chunk)[None, :]

    bank = total = None
    by_chunk = delays.reshape(beam_count, chunks, per_chunk, trials)
    for chunk in range(chunks):
        table = dft_rows((first_of + chunk * per_chunk).reshape(-1), samples)
        table = table.reshape(devices, per_chunk, 2, 2, samples)
        spectra = jnp.einsum(
            "dcoin,afin->dcoaf", table, voltages, preferred_element_type=jnp.float32
        ).astype(jnp.bfloat16)
        moved = lax.all_to_all(spectra, ("sub", "beam"), split_axis=0, concat_axis=0, tiled=True)
        power = form_beams(antenna_map, moved, weights, chunk, beam_count)
        arrived = lax.all_to_all(power, "beam", split_axis=0, concat_axis=0, tiled=True)
        last = chunk == chunks - 1
        bank, total = dedisperse(
            by_chunk[:, chunk].reshape(beam_count * per_chunk, trials), arrived, total, bank,
            chunk, chunks, out_frames, 1.0 / all_channels if last else None,
        )
    filterbank = bank.reshape(beam_count * owned, bank.shape[3], bank.shape[4])
    parts = total.reshape(sub_count, trials // sub_count, out_frames, bank.shape[3])
    parts = lax.all_to_all(parts, "sub", split_axis=0, concat_axis=0, tiled=True)
    series = jnp.sum(parts.astype(jnp.float32), axis=0).transpose(0, 2, 1)
    return (filterbank, series)


def solution(mesh):
    placed = (
        P(("sub", "beam"), None, None, None),
        P(("sub", "beam"), None, None, None),
        P(),
        P("sub", None),
    )
    return jax.shard_map(
        on_device,
        mesh=mesh,
        in_specs=placed,
        out_specs=(P("sub", "beam", None), P("sub", "beam", None)),
        check_vma=False,
    )
```

```python
import functools
import math

import jax
import jax.numpy as jnp
import numpy as np
from jax import lax
from jax.experimental import pallas as pl
from jax.experimental.pallas import tpu as pltpu
from jax.sharding import PartitionSpec as P

VMEM_BYTES = 48 * 1024 * 1024


def dft_rows(channels, samples):
    turns = (channels[:, None] * np.arange(samples)[None, :]) % samples
    phase = turns.astype(np.float32) * np.float32(2.0 * math.pi / samples)
    cosine = np.cos(phase) / math.sqrt(samples)
    sine = np.sin(phase) / math.sqrt(samples)
    real_row = np.stack([cosine, sine], axis=1)
    imag_row = np.stack([-sine, cosine], axis=1)
    return jnp.asarray(np.stack([real_row, imag_row], axis=1).astype(np.float32), jnp.bfloat16)


def beam_kernel(map_ref, x_ref, w_ref, out_ref, select, ordered):
    antennas = select.shape[0]
    frames = x_ref.shape[-1]

    @pl.when((pl.program_id(0) == 0) & (pl.program_id(1) == 0))
    def _():
        wanted = lax.broadcasted_iota(jnp.int32, (antennas, antennas), 0)
        select[...] = (wanted == map_ref[...]).astype(jnp.bfloat16)

    @pl.when(pl.program_id(1) == 0)
    def _():
        for part in range(2):
            rows = x_ref[:, 0, part].reshape(antennas, frames)
            ordered[:, part * frames:(part + 1) * frames] = jnp.dot(
                select[...], rows, preferred_element_type=jnp.float32
            ).astype(jnp.bfloat16)

    by_re = jnp.dot(w_ref[0, 0], ordered[...], preferred_element_type=jnp.float32)
    by_im = jnp.dot(w_ref[0, 1], ordered[...], preferred_element_type=jnp.float32)
    beam_re = by_re[:, :frames] - by_im[:, frames:]
    beam_im = by_re[:, frames:] + by_im[:, :frames]
    power = (beam_re * beam_re + beam_im * beam_im).astype(out_ref.dtype)
    out_ref[...] = power.reshape(out_ref.shape)


def form_beams(antenna_map, moved, weights, chunk, beam_count):
    senders, channels, _, local, frames = moved.shape
    antennas = senders * local
    beams = weights.shape[2]
    per_owner = beams // beam_count
    owners_step = min(beam_count, max(1, 512 // per_owner))
    rows = owners_step * per_owner
    flops = channels * (2 * antennas * antennas * 2 * frames + 4 * beams * antennas * 2 * frames)
    nbytes = channels * (4 * beams * antennas + 4 * antennas * frames + 2 * beams * frames)
    return pl.pallas_call(
        beam_kernel,
        grid=(channels, beams // rows),
        in_specs=[
            pl.BlockSpec((1, antennas), lambda c, b: (0, 0)),
            pl.BlockSpec((senders, 1, 2, local, frames), lambda c, b: (0, c, 0, 0, 0)),
            pl.BlockSpec((1, 2, rows, antennas), lambda c, b: (chunk * channels + c, 0, b, 0)),
        ],
        out_specs=pl.BlockSpec((owners_step, 1, per_owner, frames), lambda c, b: (b, c, 0, 0)),
        out_shape=jax.ShapeDtypeStruct((beam_count, channels, per_owner, frames), jnp.bfloat16),
        scratch_shapes=[
            pltpu.VMEM((antennas, antennas), jnp.bfloat16),
            pltpu.VMEM((antennas, 2 * frames), jnp.bfloat16),
        ],
        compiler_params=pltpu.CompilerParams(vmem_limit_bytes=VMEM_BYTES),
        cost_estimate=pl.CostEstimate(flops=flops, bytes_accessed=nbytes, transcendentals=0),
        name="form_beams",
    )(antenna_map.reshape(1, antennas), moved, weights)


def dedisperse_kernel(first, delays_ref, x_ref, *refs):
    if first:
        bank_ref, total_ref, turned = refs
        earlier = None
    else:
        earlier, _, bank_ref, total_ref, turned = refs
    senders, channels = x_ref.shape[:2]
    trials, out_frames = total_ref.shape[:2]
    bank_ref[:, 0] = x_ref[...]

    @pl.loop(0, senders)
    def _(sender):
        for channel in range(channels):
            turned[sender * channels + channel] = x_ref[sender, channel].astype(jnp.float32).T

    @pl.loop(0, trials)
    def _(trial):
        total = None if first else earlier[trial]
        for index in range(senders * channels):
            piece = turned[index, pl.ds(delays_ref[index, trial], out_frames), :]
            total = piece if total is None else total + piece
        total_ref[trial] = total


def dedisperse(delays, power, earlier, bank, chunk, chunks, out_frames):
    senders, channels, beams, frames = power.shape
    trials = delays.shape[1]
    first = earlier is None
    whole = lambda: pl.BlockSpec(memory_space=pltpu.VMEM)
    bank_block = pl.BlockSpec((senders, 1, channels, beams, frames), lambda i: (0, chunk, 0, 0, 0))
    operands = [delays, power] + ([] if first else [earlier, bank])
    in_specs = [pl.BlockSpec(memory_space=pltpu.SMEM), whole()]
    if not first:
        in_specs += [whole(), pl.BlockSpec(memory_space=pl.ANY)]
    work = senders * channels * trials * out_frames * beams
    return pl.pallas_call(
        functools.partial(dedisperse_kernel, first),
        grid=(1,),
        in_specs=in_specs,
        out_specs=[bank_block, whole()],
        out_shape=[
            jax.ShapeDtypeStruct((senders, chunks, channels, beams, frames), jnp.bfloat16),
            jax.ShapeDtypeStruct((trials, out_frames, beams), jnp.float32),
        ],
        scratch_shapes=[pltpu.VMEM((senders * channels, frames, beams), jnp.float32)],
        input_output_aliases={} if first else {3: 0},
        compiler_params=pltpu.CompilerParams(vmem_limit_bytes=VMEM_BYTES),
        cost_estimate=pl.CostEstimate(flops=4 * work, bytes_accessed=4 * 1024 * 1024, transcendentals=0),
        name="dedisperse",
    )(*operands)


def finish_kernel(scale, devices, delays_ref, x_ref, earlier, out_ref, turned, own, outgoing, incoming, sent, received):
    senders, channels = x_ref.shape[:2]
    share, out_frames = own.shape[:2]
    me = lax.axis_index("sub")
    barrier = pltpu.get_barrier_semaphore()
    for step in range(1, devices):
        pl.semaphore_signal(
            barrier, inc=1, device_id={"sub": lax.rem(me + step, devices)}, device_id_type=pl.DeviceIdType.MESH
        )

    @pl.loop(0, senders)
    def _(sender):
        for channel in range(channels):
            turned[sender * channels + channel] = x_ref[sender, channel].astype(jnp.float32).T

    def total_of(trial):
        total = earlier[trial]
        for index in range(senders * channels):
            total = total + turned[index, pl.ds(delays_ref[index, trial], out_frames), :]
        return total * scale

    pl.semaphore_wait(barrier, devices - 1)
    copies = []
    for step in range(1, devices):
        peer = lax.rem(me + step, devices)

        @pl.loop(0, share)
        def _(trial):
            outgoing[step - 1, trial] = total_of(peer * share + trial).astype(outgoing.dtype)

        copy = pltpu.make_async_remote_copy(
            src_ref=outgoing.at[step - 1],
            dst_ref=incoming.at[step - 1],
            send_sem=sent.at[step - 1],
            recv_sem=received.at[step - 1],
            device_id={"sub": peer},
            device_id_type=pl.DeviceIdType.MESH,
        )
        copy.start()
        copies.append(copy)

    @pl.loop(0, share)
    def _(trial):
        own[trial] = total_of(me * share + trial)

    for copy in copies:
        copy.wait()

    @pl.loop(0, share)
    def _(trial):
        total = own[trial]
        for step in range(devices - 1):
            total = total + incoming[step, trial].astype(jnp.float32)
        out_ref[trial] = total.T


def finish(delays, power, earlier, scale):
    senders, channels, beams, frames = power.shape
    trials, out_frames = earlier.shape[:2]
    devices = lax.axis_size("sub")
    share = trials // devices
    in_vmem = pl.BlockSpec(memory_space=pltpu.VMEM)
    work = senders * channels * trials * out_frames * beams
    return pl.pallas_call(
        functools.partial(finish_kernel, scale, devices),
        in_specs=[pl.BlockSpec(memory_space=pltpu.SMEM), in_vmem, in_vmem],
        out_specs=in_vmem,
        out_shape=jax.ShapeDtypeStruct((share, beams, out_frames), jnp.float32),
        scratch_shapes=[
            pltpu.VMEM((senders * channels, frames, beams), jnp.float32),
            pltpu.VMEM((share, out_frames, beams), jnp.float32),
            pltpu.VMEM((devices - 1, share, out_frames, beams), jnp.bfloat16),
            pltpu.VMEM((devices - 1, share, out_frames, beams), jnp.bfloat16),
            pltpu.SemaphoreType.DMA((devices - 1,)),
            pltpu.SemaphoreType.DMA((devices - 1,)),
        ],
        compiler_params=pltpu.CompilerParams(
            vmem_limit_bytes=VMEM_BYTES, collective_id=0, has_side_effects=True
        ),
        cost_estimate=pl.CostEstimate(flops=4 * work, bytes_accessed=4 * 1024 * 1024, transcendentals=0),
        name="finish_series",
    )(delays, power, earlier)


def on_device(voltages, weights, antenna_map, delays):
    samples = voltages.shape[3]
    sub_count = lax.axis_size("sub")
    beam_count = lax.axis_size("beam")
    devices = sub_count * beam_count
    owned = weights.shape[0]
    all_channels = owned * devices
    trials = delays.shape[1]
    out_frames = voltages.shape[1] // 2
    chunks = min(2, owned)
    per_chunk = owned // chunks
    first_of = np.arange(devices)[:, None] * owned + np.arange(per_chunk)[None, :]

    bank = total = None
    by_chunk = delays.reshape(beam_count, chunks, per_chunk, trials)
    for chunk in range(chunks):
        table = dft_rows((first_of + chunk * per_chunk).reshape(-1), samples)
        table = table.reshape(devices, per_chunk, 2, 2, samples)
        spectra = jnp.einsum(
            "dcoin,afin->dcoaf", table, voltages, preferred_element_type=jnp.float32
        ).astype(jnp.bfloat16)
        moved = lax.all_to_all(spectra, ("sub", "beam"), split_axis=0, concat_axis=0, tiled=True)
        power = form_beams(antenna_map, moved, weights, chunk, beam_count)
        arrived = lax.all_to_all(power, "beam", split_axis=0, concat_axis=0, tiled=True)
        shifts = by_chunk[:, chunk].reshape(beam_count * per_chunk, trials)
        if chunk < chunks - 1:
            bank, total = dedisperse(shifts, arrived, total, bank, chunk, chunks, out_frames)
        else:
            bank = lax.dynamic_update_slice(bank, arrived[:, None], (0, chunk, 0, 0, 0))
            series = finish(shifts, arrived, total, 1.0 / all_channels)
    filterbank = bank.reshape(beam_count * owned, bank.shape[3], bank.shape[4])
    return (filterbank, series)


def solution(mesh):
    placed = (
        P(("sub", "beam"), None, None, None),
        P(("sub", "beam"), None, None, None),
        P(),
        P("sub", None),
    )
    return jax.shard_map(
        on_device,
        mesh=mesh,
        in_specs=placed,
        out_specs=(P("sub", "beam", None), P("sub", "beam", None)),
        check_vma=False,
    )
```

```python
import functools
import math

import jax
import jax.numpy as jnp
import numpy as np
from jax import lax
from jax.experimental import pallas as pl
from jax.experimental.pallas import tpu as pltpu
from jax.sharding import PartitionSpec as P

VMEM_BYTES = 48 * 1024 * 1024


def dft_rows(channels, samples):
    turns = (channels[..., None] * np.arange(samples)) % samples
    phase = turns.astype(np.float32) * np.float32(2.0 * math.pi / samples)
    cosine = np.cos(phase) / math.sqrt(samples)
    sine = np.sin(phase) / math.sqrt(samples)
    real_row = np.stack([cosine, sine], axis=2)
    imag_row = np.stack([-sine, cosine], axis=2)
    table = np.stack([real_row, imag_row], axis=1).astype(np.float32)
    return jnp.asarray(table.reshape(-1, 2, samples), jnp.bfloat16)


def beam_kernel(map_ref, x_ref, w_ref, out_ref, select, ordered):
    antennas = select.shape[0]
    frames = x_ref.shape[-1]

    @pl.when((pl.program_id(0) == 0) & (pl.program_id(1) == 0))
    def _():
        wanted = lax.broadcasted_iota(jnp.int32, (antennas, antennas), 0)
        select[...] = (wanted == map_ref[...]).astype(jnp.bfloat16)

    @pl.when(pl.program_id(1) == 0)
    def _():
        for part in range(2):
            rows = x_ref[:, 0, part].reshape(antennas, frames)
            ordered[:, part * frames:(part + 1) * frames] = jnp.dot(
                select[...], rows, preferred_element_type=jnp.float32
            ).astype(jnp.bfloat16)

    by_re = jnp.dot(w_ref[0, 0], ordered[...], preferred_element_type=jnp.float32)
    by_im = jnp.dot(w_ref[0, 1], ordered[...], preferred_element_type=jnp.float32)
    beam_re = by_re[:, :frames] - by_im[:, frames:]
    beam_im = by_re[:, frames:] + by_im[:, :frames]
    power = (beam_re * beam_re + beam_im * beam_im).astype(out_ref.dtype)
    out_ref[...] = power.reshape(out_ref.shape)


def form_beams(antenna_map, moved, weights, chunk, beam_count):
    senders, channels, _, local, frames = moved.shape
    antennas = senders * local
    beams = weights.shape[2]
    per_owner = beams // beam_count
    owners_step = min(beam_count, max(1, 512 // per_owner))
    rows = owners_step * per_owner
    flops = channels * (2 * antennas * antennas * 2 * frames + 4 * beams * antennas * 2 * frames)
    nbytes = channels * (4 * beams * antennas + 4 * antennas * frames + 2 * beams * frames)
    return pl.pallas_call(
        beam_kernel,
        grid=(channels, beams // rows),
        in_specs=[
            pl.BlockSpec((1, antennas), lambda c, b: (0, 0)),
            pl.BlockSpec((senders, 1, 2, local, frames), lambda c, b: (0, c, 0, 0, 0)),
            pl.BlockSpec((1, 2, rows, antennas), lambda c, b: (chunk * channels + c, 0, b, 0)),
        ],
        out_specs=pl.BlockSpec((owners_step, 1, per_owner, frames), lambda c, b: (b, c, 0, 0)),
        out_shape=jax.ShapeDtypeStruct((beam_count, channels, per_owner, frames), jnp.bfloat16),
        scratch_shapes=[
            pltpu.VMEM((antennas, antennas), jnp.bfloat16),
            pltpu.VMEM((antennas, 2 * frames), jnp.bfloat16),
        ],
        compiler_params=pltpu.CompilerParams(vmem_limit_bytes=VMEM_BYTES),
        cost_estimate=pl.CostEstimate(flops=flops, bytes_accessed=nbytes, transcendentals=0),
        name="form_beams",
    )(antenna_map.reshape(1, antennas), moved, weights)


def dedisperse_kernel(first, delays_ref, x_ref, *refs):
    if first:
        bank_ref, total_ref, turned = refs
        earlier = None
    else:
        earlier, _, bank_ref, total_ref, turned = refs
    senders, channels = x_ref.shape[:2]
    trials, out_frames = total_ref.shape[:2]
    bank_ref[:, 0] = x_ref[...]

    @pl.loop(0, senders)
    def _(sender):
        for channel in range(channels):
            turned[sender * channels + channel] = x_ref[sender, channel].astype(jnp.float32).T

    @pl.loop(0, trials)
    def _(trial):
        total = None if first else earlier[trial]
        for index in range(senders * channels):
            piece = turned[index, pl.ds(delays_ref[index, trial], out_frames), :]
            total = piece if total is None else total + piece
        total_ref[trial] = total


def dedisperse(delays, power, earlier, bank, chunk, chunks, out_frames):
    senders, channels, beams, frames = power.shape
    trials = delays.shape[1]
    first = earlier is None
    whole = lambda: pl.BlockSpec(memory_space=pltpu.VMEM)
    bank_block = pl.BlockSpec((senders, 1, channels, beams, frames), lambda i: (0, chunk, 0, 0, 0))
    operands = [delays, power] + ([] if first else [earlier, bank])
    in_specs = [pl.BlockSpec(memory_space=pltpu.SMEM), whole()]
    if not first:
        in_specs += [whole(), pl.BlockSpec(memory_space=pl.ANY)]
    work = senders * channels * trials * out_frames * beams
    return pl.pallas_call(
        functools.partial(dedisperse_kernel, first),
        grid=(1,),
        in_specs=in_specs,
        out_specs=[bank_block, whole()],
        out_shape=[
            jax.ShapeDtypeStruct((senders, chunks, channels, beams, frames), jnp.bfloat16),
            jax.ShapeDtypeStruct((trials, out_frames, beams), jnp.float32),
        ],
        scratch_shapes=[pltpu.VMEM((senders * channels, frames, beams), jnp.float32)],
        input_output_aliases={} if first else {3: 0},
        compiler_params=pltpu.CompilerParams(vmem_limit_bytes=VMEM_BYTES),
        cost_estimate=pl.CostEstimate(flops=4 * work, bytes_accessed=4 * 1024 * 1024, transcendentals=0),
        name="dedisperse",
    )(*operands)


def finish_kernel(scale, devices, delays_ref, x_ref, earlier, out_ref, turned, own, outgoing, incoming, sent, received):
    senders, channels = x_ref.shape[:2]
    share, out_frames = own.shape[:2]
    me = lax.axis_index("sub")
    barrier = pltpu.get_barrier_semaphore()
    for step in range(1, devices):
        pl.semaphore_signal(
            barrier, inc=1, device_id={"sub": lax.rem(me + step, devices)}, device_id_type=pl.DeviceIdType.MESH
        )

    @pl.loop(0, senders)
    def _(sender):
        for channel in range(channels):
            turned[sender * channels + channel] = x_ref[sender, channel].astype(jnp.float32).T

    def total_of(trial):
        total = earlier[trial]
        for index in range(senders * channels):
            total = total + turned[index, pl.ds(delays_ref[index, trial], out_frames), :]
        return total * scale

    pl.semaphore_wait(barrier, devices - 1)
    copies = []
    for step in range(1, devices):
        peer = lax.rem(me + step, devices)

        @pl.loop(0, share)
        def _(trial):
            outgoing[step - 1, trial] = total_of(peer * share + trial).astype(outgoing.dtype)

        copy = pltpu.make_async_remote_copy(
            src_ref=outgoing.at[step - 1],
            dst_ref=incoming.at[step - 1],
            send_sem=sent.at[step - 1],
            recv_sem=received.at[step - 1],
            device_id={"sub": peer},
            device_id_type=pl.DeviceIdType.MESH,
        )
        copy.start()
        copies.append(copy)

    @pl.loop(0, share)
    def _(trial):
        own[trial] = total_of(me * share + trial)

    for copy in copies:
        copy.wait()

    @pl.loop(0, share)
    def _(trial):
        total = own[trial]
        for step in range(devices - 1):
            total = total + incoming[step, trial].astype(jnp.float32)
        out_ref[trial] = total.T


def finish(delays, power, earlier, scale):
    senders, channels, beams, frames = power.shape
    trials, out_frames = earlier.shape[:2]
    devices = lax.axis_size("sub")
    share = trials // devices
    in_vmem = pl.BlockSpec(memory_space=pltpu.VMEM)
    work = senders * channels * trials * out_frames * beams
    return pl.pallas_call(
        functools.partial(finish_kernel, scale, devices),
        in_specs=[pl.BlockSpec(memory_space=pltpu.SMEM), in_vmem, in_vmem],
        out_specs=in_vmem,
        out_shape=jax.ShapeDtypeStruct((share, beams, out_frames), jnp.float32),
        scratch_shapes=[
            pltpu.VMEM((senders * channels, frames, beams), jnp.float32),
            pltpu.VMEM((share, out_frames, beams), jnp.float32),
            pltpu.VMEM((devices - 1, share, out_frames, beams), jnp.bfloat16),
            pltpu.VMEM((devices - 1, share, out_frames, beams), jnp.bfloat16),
            pltpu.SemaphoreType.DMA((devices - 1,)),
            pltpu.SemaphoreType.DMA((devices - 1,)),
        ],
        compiler_params=pltpu.CompilerParams(
            vmem_limit_bytes=VMEM_BYTES, collective_id=0, has_side_effects=True
        ),
        cost_estimate=pl.CostEstimate(flops=4 * work, bytes_accessed=4 * 1024 * 1024, transcendentals=0),
        name="finish_series",
    )(delays, power, earlier)


def on_device(voltages, weights, antenna_map, delays):
    samples = voltages.shape[3]
    sub_count = lax.axis_size("sub")
    beam_count = lax.axis_size("beam")
    devices = sub_count * beam_count
    owned = weights.shape[0]
    all_channels = owned * devices
    trials = delays.shape[1]
    out_frames = voltages.shape[1] // 2
    chunks = min(2, owned)
    per_chunk = owned // chunks
    first_of = np.arange(devices)[:, None] * owned + np.arange(per_chunk)[None, :]

    bank = total = None
    by_chunk = delays.reshape(beam_count, chunks, per_chunk, trials)
    for chunk in range(chunks):
        table = dft_rows((first_of + chunk * per_chunk).T, samples)
        spectra = jnp.einsum(
            "rin,afin->arf", table, voltages, preferred_element_type=jnp.float32
        ).astype(jnp.bfloat16)
        spectra = spectra.reshape(spectra.shape[0], per_chunk, 2, devices, spectra.shape[2])
        spectra = spectra.transpose(3, 1, 2, 0, 4)
        moved = lax.all_to_all(spectra, ("sub", "beam"), split_axis=0, concat_axis=0, tiled=True)
        power = form_beams(antenna_map, moved, weights, chunk, beam_count)
        arrived = lax.all_to_all(power, "beam", split_axis=0, concat_axis=0, tiled=True)
        shifts = by_chunk[:, chunk].reshape(beam_count * per_chunk, trials)
        if chunk < chunks - 1:
            bank, total = dedisperse(shifts, arrived, total, bank, chunk, chunks, out_frames)
        else:
            bank = lax.dynamic_update_slice(bank, arrived[:, None], (0, chunk, 0, 0, 0))
            series = finish(shifts, arrived, total, 1.0 / all_channels)
    filterbank = bank.reshape(beam_count * owned, bank.shape[3], bank.shape[4])
    return (filterbank, series)


def solution(mesh):
    placed = (
        P(("sub", "beam"), None, None, None),
        P(("sub", "beam"), None, None, None),
        P(),
        P("sub", None),
    )
    return jax.shard_map(
        on_device,
        mesh=mesh,
        in_specs=placed,
        out_specs=(P("sub", "beam", None), P("sub", "beam", None)),
        check_vma=False,
    )
```
